32 devices in a mesh: head: 2 (over y), ctx: 16 (over z, x, core).
Axes of the slice: x: 2, y: 2, z: 4, core: 2. Of those that a mesh axis runs over, the one named last changes fastest.
Arguments:
- queries: bfloat16 [8192, 64, 128], P(('ctx', 'head')), may hold values from -6 to 6
- keys: bfloat16 [8192, 8, 128], P(('ctx', 'head')), may hold values from -6 to 6
- values: bfloat16 [8192, 8, 128], P(('ctx', 'head')), may hold values from -6 to 6
- out_grad: bfloat16 [8192, 64, 128], P(('ctx', 'head')), may hold values from -6 to 6
- doc_lengths: int32 [48], replicated, may hold values from 1 to 1024, 8192 in all
- stored_block_order: int32 [64], replicated, may hold values from 0 to 63, as said below
Outputs:
- attended: bfloat16 [8192, 64, 128], P(('ctx', 'head'))
- query_grad: bfloat16 [8192, 64, 128], P(('ctx', 'head'))
- key_gradient: bfloat16 [8192, 8, 128], P(('ctx', 'head'))
- value_gradient: bfloat16 [8192, 8, 128], P(('ctx', 'head'))
The draws below stay inside these ranges and needn't reach their ends.
Inputs may be any that keep to these rules, and one draw needn't show every extreme that they name: `doc_lengths`: they sum to 8192 and the largest is exactly 1024. A permutation in which stored_block_order[b] // 4 = b // 4: the stored blocks of each aligned group of 4 are that group's sequence blocks in some order.
All inputs are finite; a program needn't handle non-finite values.
Results may differ from the reference program's by a relative error of at most 0.039.
Values may be sent and summed in bfloat16 or wider, within the bound.
A program may use at most 192 MiB of HBM per device.

```python
import math
import jax
import jax.numpy as jnp
import numpy as np
from jax import lax

QUERY_HEADS = 64
KEY_VALUE_HEADS = 8
HEAD_SIZE = 128
BLOCK_TOKENS = 128
BLK_DEV = 4
DOCS = 48
STORED_BLOCKS = 64
SEQUENCE_TOKENS = 8192
DOC_MOST = 1024


def shared_keys(key):
    key_offset_base = jax.random.fold_in(key, 0)
    unpermuted_keys = jnp.clip(jax.random.normal(key_offset_base, (SEQUENCE_TOKENS, KEY_VALUE_HEADS, HEAD_SIZE), jnp.float32), -5.5, 5.5)
    return unpermuted_keys


def draw_keys(key, part):
    unpermuted_keys = shared_keys(key)
    return unpermuted_keys.astype(jnp.bfloat16)


def draw_queries(key, part):
    key = jax.random.fold_in(key, 5)
    drawn_rows = jnp.clip(jax.random.normal(key, (SEQUENCE_TOKENS, QUERY_HEADS, HEAD_SIZE), jnp.float32), -5.5, 5.5)
    return drawn_rows.astype(jnp.bfloat16)


def draw_stored_block_order(key, part):
    key = jax.random.fold_in(key, 7)
    groups = STORED_BLOCKS // BLK_DEV
    group_keys = jax.random.split(key, groups)
    shuffled = jax.vmap(lambda one_key: jax.random.permutation(one_key, BLK_DEV))(group_keys).astype(jnp.int32)
    starts = jnp.arange(groups, dtype=jnp.int32)[:, None] * BLK_DEV
    return (starts + shuffled).reshape(STORED_BLOCKS).astype(jnp.int32)


def steps_of(own_key, dims, pieces, low, high):
    def one(position, blocks):
        draws = jax.random.uniform(jax.random.fold_in(jax.random.fold_in(own_key, 6), position), (blocks,), jnp.float32, low / len(pieces), high / len(pieces))
        return jnp.repeat(jnp.exp(draws), dims[position] // blocks).reshape((-1,) + (1,) * (len(dims) - position - 1))

    level = one(*pieces[0])
    for cut in pieces[1:]:
        level = level * one(*cut)
    return level


def profile(count, total, reach, skew):
    portions = [(1 << 20) // math.isqrt(rank ** skew) + 1 for rank in range(2, count + 1)]
    rest, given = total - reach - (count - 1), [1] * (count - 1)
    while rest > 0:
        candidates = [i for i in range(count - 1) if given[i] < reach]
        whole, left = sum([portions[i] for i in candidates]), rest
        for i in candidates:
            more = min(reach - given[i], max(1, left * portions[i] // whole), rest)
            given[i] = given[i] + more
            rest = rest - more
    return np.array([reach] + given)


def ragged_sizes(own_key, number_of, total, reach, skew):
    if number_of == 2:
        one = jax.random.randint(own_key, (), max(1, total - reach), min(reach, total - 1) + 1)
        return jnp.stack([one, total - one])
    tallies = jnp.asarray(profile(number_of, total, reach, skew), jnp.int32)
    twos = (number_of - 1) // 2
    giver, sink = tallies[1:1 + 2 * twos:2], tallies[2:2 + 2 * twos:2]
    margin = jnp.minimum(giver - 1, reach - sink)
    passed = jax.random.randint(jax.random.fold_in(own_key, 1), (twos,), 0, 1 << 20) % (margin + 1)
    tallies = tallies.at[1:1 + 2 * twos:2].set(giver - passed).at[2:2 + 2 * twos:2].set(sink + passed)
    return tallies[jax.random.permutation(jax.random.fold_in(own_key, 2), number_of)]


def bell_draw(key, shape, scale, most, pieces=(), kind=jnp.bfloat16):
    array = jax.random.normal(key, shape, jnp.float32) * scale
    if len(pieces) > 0:
        array = steps_of(key, shape, pieces, -0.22, 0.18) * array
    return jnp.clip(array, min=-most, max=most).astype(kind)


def setup_inputs(seed: int = 0) -> dict:
    splits = jax.random.split(jax.random.key(seed), 7)
    queries = draw_queries(jax.random.fold_in(splits[6], 71), 0)
    keys = draw_keys(jax.random.fold_in(splits[6], 71), 0)
    values = bell_draw(splits[2], (SEQUENCE_TOKENS, KEY_VALUE_HEADS, HEAD_SIZE), 1.0, 6.0, ((0, 32),))
    out_grad = bell_draw(splits[3], (SEQUENCE_TOKENS, QUERY_HEADS, HEAD_SIZE), 1.0, 6.0, ((0, 32),))
    doc_lengths = ragged_sizes(splits[4], DOCS, SEQUENCE_TOKENS, DOC_MOST, 2).astype(jnp.int32)
    stored_block_order = draw_stored_block_order(jax.random.fold_in(splits[6], 71), 0)
    return dict(queries=queries, keys=keys, values=values, out_grad=out_grad, doc_lengths=doc_lengths, stored_block_order=stored_block_order)


neg_big = -1.0e30


def segment_ids(positions, doc_lengths):
    ends = jnp.cumsum(doc_lengths).astype(jnp.int32)
    return jnp.sum((positions[..., None] >= ends).astype(jnp.int32), axis=-1).astype(jnp.int32)


def lowered(values_in):
    return lax.optimization_barrier(values_in.astype(jnp.bfloat16)).astype(jnp.float32)


def reference(queries, keys, values, out_grad, doc_lengths, stored_block_order):
    score_scale = HEAD_SIZE ** -0.5
    sharing_count = QUERY_HEADS // KEY_VALUE_HEADS
    window_blocks = DOC_MOST // BLOCK_TOKENS + 1
    window_rows = window_blocks * BLOCK_TOKENS
    inverse = jnp.zeros((STORED_BLOCKS,), jnp.int32).at[stored_block_order].set(jnp.arange(STORED_BLOCKS, dtype=jnp.int32))

    def in_order(blocked_array):
        shaped = blocked_array.reshape((STORED_BLOCKS, BLOCK_TOKENS) + blocked_array.shape[1:])
        return shaped[inverse].reshape(blocked_array.shape)

    query_sequence = in_order(queries)
    key_seq = in_order(keys)
    value_seq = in_order(values)
    gradient_sequence = in_order(out_grad)
    doc_ids = segment_ids(jnp.arange(SEQUENCE_TOKENS, dtype=jnp.int32), doc_lengths)

    def block_step(running, block_index):
        key_accumulator, value_accumulator = running
        row_offset_start = (block_index * BLOCK_TOKENS).astype(jnp.int32)
        key_start = (jnp.clip(block_index + 1 - window_blocks, 0, STORED_BLOCKS - window_blocks) * BLOCK_TOKENS).astype(jnp.int32)
        query_block_rows = lax.dynamic_slice_in_dim(query_sequence, row_offset_start, BLOCK_TOKENS, 0).astype(jnp.float32).reshape(BLOCK_TOKENS, KEY_VALUE_HEADS, sharing_count, HEAD_SIZE)
        gradient_block = lax.dynamic_slice_in_dim(gradient_sequence, row_offset_start, BLOCK_TOKENS, 0).astype(jnp.float32).reshape(BLOCK_TOKENS, KEY_VALUE_HEADS, sharing_count, HEAD_SIZE)
        key_window = lax.dynamic_slice_in_dim(key_seq, key_start, window_rows, 0).astype(jnp.float32)
        value_window = lax.dynamic_slice_in_dim(value_seq, key_start, window_rows, 0).astype(jnp.float32)
        query_pos = row_offset_start + jnp.arange(BLOCK_TOKENS, dtype=jnp.int32)
        key_pos = key_start + jnp.arange(window_rows, dtype=jnp.int32)
        query_doc = lax.dynamic_slice_in_dim(doc_ids, row_offset_start, BLOCK_TOKENS, 0)
        key_doc = lax.dynamic_slice_in_dim(doc_ids, key_start, window_rows, 0)
        allowed = (query_doc[:, None] == key_doc[None, :]) & (key_pos[None, :] <= query_pos[:, None])
        scores = jnp.einsum("qhgd,khd->hgqk", query_block_rows, key_window) * score_scale
        row_max = jnp.max(jnp.where(allowed, scores, neg_big), axis=-1)
        row_total = jnp.sum(jnp.where(allowed, jnp.exp(scores - row_max[..., None]), 0.0), axis=-1)
        log_total = row_max + jnp.log(row_total)
        weights = jnp.where(allowed, jnp.exp(scores - log_total[..., None]), 0.0)
        weights_low = lowered(weights)
        attended_block = jnp.einsum("hgqk,khd->qhgd", weights_low, value_window).astype(jnp.bfloat16)
        row_delta = jnp.sum(gradient_block * attended_block.astype(jnp.float32), axis=-1).transpose(1, 2, 0)
        grad_weights = jnp.einsum("qhgd,khd->hgqk", gradient_block, value_window)
        grad_scores = lowered(weights * (grad_weights - row_delta[..., None]))
        query_part = jnp.einsum("hgqk,khd->qhgd", grad_scores, key_window) * score_scale
        key_part = jnp.einsum("hgqk,qhgd->khd", grad_scores, query_block_rows) * score_scale
        value_part = jnp.einsum("hgqk,qhgd->khd", weights_low, gradient_block)
        key_accumulator = lax.dynamic_update_slice_in_dim(key_accumulator, lax.dynamic_slice_in_dim(key_accumulator, key_start, window_rows, 0) + key_part, key_start, 0)
        value_accumulator = lax.dynamic_update_slice_in_dim(value_accumulator, lax.dynamic_slice_in_dim(value_accumulator, key_start, window_rows, 0) + value_part, key_start, 0)
        outputs = (attended_block.reshape(BLOCK_TOKENS, QUERY_HEADS, HEAD_SIZE), query_part.reshape(BLOCK_TOKENS, QUERY_HEADS, HEAD_SIZE).astype(jnp.bfloat16))
        return (key_accumulator, value_accumulator), outputs

    initial_accumulator = (jnp.zeros((SEQUENCE_TOKENS, KEY_VALUE_HEADS, HEAD_SIZE), jnp.float32), jnp.zeros((SEQUENCE_TOKENS, KEY_VALUE_HEADS, HEAD_SIZE), jnp.float32))
    (key_accumulator, value_accumulator), (attended_pos, query_pos_grad) = lax.scan(block_step, initial_accumulator, jnp.arange(STORED_BLOCKS, dtype=jnp.int32))
    attended = attended_pos[stored_block_order].reshape(SEQUENCE_TOKENS, QUERY_HEADS, HEAD_SIZE)
    query_grad = query_pos_grad[stored_block_order].reshape(SEQUENCE_TOKENS, QUERY_HEADS, HEAD_SIZE)
    key_gradient = key_accumulator.reshape(STORED_BLOCKS, BLOCK_TOKENS, KEY_VALUE_HEADS, HEAD_SIZE)[stored_block_order].reshape(SEQUENCE_TOKENS, KEY_VALUE_HEADS, HEAD_SIZE).astype(jnp.bfloat16)
    value_gradient = value_accumulator.reshape(STORED_BLOCKS, BLOCK_TOKENS, KEY_VALUE_HEADS, HEAD_SIZE)[stored_block_order].reshape(SEQUENCE_TOKENS, KEY_VALUE_HEADS, HEAD_SIZE).astype(jnp.bfloat16)
    return attended, query_grad, key_gradient, value_gradient
```

```python
import functools
import math

import jax
import jax.numpy as jnp
from jax import lax
from jax.experimental import pallas as pl
from jax.experimental.pallas import tpu as pltpu
from jax.sharding import PartitionSpec as P

HEAD_SIZE = 128
BLOCK_TOKENS = 128
HOPS = 2
DOC_MOST = 1024
CHUNKS = 4
NEG_BIG = -1e30
SCALE = HEAD_SIZE ** (-0.5)
SCALE_LOG2 = SCALE * math.log2(math.e)

NN = (((1,), (0,)), ((), ()))
NT = (((1,), (1,)), ((), ()))
TN = (((0,), (0,)), ((), ()))


def dot(a, b, dims):
    return lax.dot_general(a, b, dims, preferred_element_type=jnp.float32)


def attention_kernel(slot_ref, span_ref, info_ref, q_ref, g_ref, kv_ref, *rest):
    (o_ref, dq_ref, dkv_ref, s_scr, e_scr, oT, dqT, dkv_acc) = rest[-8:]
    turn = pl.program_id(1)
    bt, share = q_ref.shape[:2]
    rows = bt * share

    @pl.when(turn == 0)
    def _():
        dkv_acc[...] = jnp.zeros_like(dkv_acc)

    last = span_ref[2 * turn]
    tiles = span_ref[2 * turn + 1]
    query = q_ref[...].reshape(rows, HEAD_SIZE)
    start = info_ref[0, 0:1, :]
    place = info_ref[0, 1:2, :]

    def slots(t):
        high = last - 2 * t
        return slot_ref[jnp.maximum(high - 1, 0)], slot_ref[high]

    def tile_of(which, t):
        low, high = slots(t)
        return jnp.concatenate([kv_ref[0, which, low], kv_ref[0, which, high]], axis=0)

    def scores(t, diagonal):
        s = dot(tile_of(0, t), query, NT)
        kpos = (last - 2 * t - 1) * bt + lax.broadcasted_iota(jnp.int32, (2 * bt, 1), 0)
        keep = kpos >= start
        if diagonal:
            keep = keep & (kpos <= place)
        s = jnp.where(keep, s, NEG_BIG)
        s_scr[t] = s
        return jnp.max(s.reshape(2 * bt // 8, 8, rows), axis=0)

    m8 = scores(0, True)
    m8 = lax.fori_loop(1, tiles, lambda t, m: jnp.maximum(m, scores(t, False)), m8)
    top = jnp.max(m8, axis=0, keepdims=True) * SCALE_LOG2

    oT[...] = jnp.zeros_like(oT)

    def weights(t, total):
        e = jnp.exp2(s_scr[t] * SCALE_LOG2 - top)
        low = e.astype(jnp.bfloat16)
        e_scr[t] = low
        oT[...] += dot(tile_of(1, t), low, TN)
        return total + jnp.sum(e.reshape(2 * bt // 8, 8, rows), axis=0)

    l8 = lax.fori_loop(0, tiles, weights, jnp.zeros((8, rows), jnp.float32))
    inv = 1.0 / jnp.sum(l8, axis=0, keepdims=True)
    out_t = oT[...] * inv
    o_ref[...] = out_t.T.astype(jnp.bfloat16).reshape(q_ref.shape)
    out_t = out_t.astype(jnp.bfloat16).astype(jnp.float32)
    grad_t = (g_ref[...].reshape(rows, HEAD_SIZE).astype(jnp.float32).T * inv).astype(jnp.bfloat16)
    grad_f = grad_t.astype(jnp.float32)
    delta = jnp.sum(grad_f * out_t, axis=0, keepdims=True)
    grad = grad_f.T.astype(jnp.bfloat16)

    dqT[...] = jnp.zeros_like(dqT)

    def back(t, carry):
        low, high = slots(t)
        e = e_scr[t]
        dp = dot(tile_of(1, t), grad_t, NN)
        ds = (e.astype(jnp.float32) * (dp - delta)).astype(jnp.bfloat16)
        dqT[...] += dot(tile_of(0, t), ds, TN)
        dk = dot(ds, query, NN)
        dv = dot(e, grad, NN)
        dkv_acc[0, low] += dk[:bt]
        dkv_acc[0, high] += dk[bt:]
        dkv_acc[1, low] += dv[:bt]
        dkv_acc[1, high] += dv[bt:]
        return carry

    lax.fori_loop(0, tiles, back, 0)
    dq_ref[...] = (dqT[...] * SCALE).T.astype(jnp.bfloat16).reshape(q_ref.shape)

    @pl.when(turn == pl.num_programs(1) - 1)
    def _():
        dkv_ref[0, 0] = (dkv_acc[0] * SCALE).astype(jnp.bfloat16)
        dkv_ref[0, 1] = dkv_acc[1].astype(jnp.bfloat16)


def attend(slot_of, spans, info, queries, out_grad, window, first_head, so_far):
    tokens, heads, _ = queries.shape
    chunk, _, wblocks = window.shape[:3]
    bt = window.shape[3]
    share = info.shape[2] // bt
    turns = tokens // bt
    rows = bt * share
    max_tiles = DOC_MOST // bt // 2 + 1
    by_head = pl.BlockSpec((bt, share, HEAD_SIZE), lambda h, i, *_: (i, first_head + h, 0))
    kv_spec = pl.BlockSpec(
        (1, 2, wblocks, bt, HEAD_SIZE), lambda h, i, *_: (h, 0, 0, 0, 0)
    )
    in_specs = [
        pl.BlockSpec((1, 2, rows), lambda h, i, *_: (i, 0, 0)),
        by_head,
        by_head,
        kv_spec,
    ]
    operands = [slot_of, spans, info, queries, out_grad, window]
    aliases = {}
    if so_far is not None:
        in_specs += [pl.BlockSpec(memory_space=pl.ANY)] * 2
        operands += list(so_far)
        aliases = {6: 0, 7: 1}
    big = jax.ShapeDtypeStruct(queries.shape, jnp.bfloat16)
    pairs = chunk * turns * rows * 6 * bt
    return pl.pallas_call(
        attention_kernel,
        grid_spec=pltpu.PrefetchScalarGridSpec(
            num_scalar_prefetch=2,
            grid=(chunk, turns),
            in_specs=in_specs,
            out_specs=[by_head, by_head, kv_spec],
            scratch_shapes=[
                pltpu.VMEM((max_tiles, 2 * bt, rows), jnp.float32),
                pltpu.VMEM((max_tiles, 2 * bt, rows), jnp.bfloat16),
                pltpu.VMEM((HEAD_SIZE, rows), jnp.float32),
                pltpu.VMEM((HEAD_SIZE, rows), jnp.float32),
                pltpu.VMEM((2, wblocks, bt, HEAD_SIZE), jnp.float32),
            ],
        ),
        out_shape=[big, big, jax.ShapeDtypeStruct(window.shape, jnp.bfloat16)],
        input_output_aliases=aliases,
        compiler_params=pltpu.CompilerParams(vmem_limit_bytes=48 * 1024 * 1024),
        cost_estimate=pl.CostEstimate(
            flops=12 * pairs * HEAD_SIZE,
            bytes_accessed=4 * chunk * tokens * share * HEAD_SIZE * 2 + 4 * window.size,
            transcendentals=pairs,
        ),
    )(*operands)


def shifted(block, axis, distance):
    size = lax.axis_size(axis)
    route = [(i - distance, i) for i in range(size) if 0 <= i - distance < size]
    return lax.ppermute(block, axis, route)


def rolled(block, axis, distance):
    size = lax.axis_size(axis)
    return lax.ppermute(block, axis, [(i, (i + distance) % size) for i in range(size)])


def body(queries, keys, values, out_grad, doc_lengths, stored_block_order):
    tokens, heads, _ = queries.shape
    bt = min(BLOCK_TOKENS, tokens)
    pieces = BLOCK_TOKENS // bt
    stored_order = stored_block_order[:, None] * pieces + jnp.arange(pieces, dtype=jnp.int32)
    stored_order = stored_order.reshape(-1)
    kv_heads = keys.shape[1]
    share = heads // kv_heads
    own_blocks = tokens // bt
    split = lax.axis_size("head")
    me_head, me_ctx = lax.axis_index("head"), lax.axis_index("ctx")
    group = own_blocks * split
    window_blocks = (HOPS + 1) * group

    w = jnp.arange(window_blocks, dtype=jnp.int32)
    hop, turn, inner = w // group, (w % group) // own_blocks, w % own_blocks
    source = lax.rem(me_head - turn + split, split)
    stored = jnp.maximum(me_ctx - hop, 0) * group + source * own_blocks + inner
    rel = (HOPS - hop) * group + stored_order[stored] % group
    slot_of = jnp.sum(jnp.where(rel[None, :] == w[:, None], w[None, :], 0), axis=1).astype(jnp.int32)

    own = (me_ctx * split + me_head) * own_blocks
    base = (me_ctx - HOPS) * group
    blocks = lax.dynamic_slice_in_dim(stored_order, own, own_blocks, 0) - base
    place = blocks[:, None] * bt + jnp.arange(bt, dtype=jnp.int32)[None, :]
    ends = jnp.cumsum(doc_lengths).astype(jnp.int32) - base * bt
    start = jnp.max(
        jnp.where(ends[None, None, :] <= place[..., None], ends[None, None, :], -base * bt), axis=-1
    )
    tiles = (blocks - start[:, 0] // bt) // 2 + 1
    spans = jnp.stack([blocks, tiles], axis=1).reshape(-1).astype(jnp.int32)
    info = jnp.repeat(jnp.stack([start, place], axis=1), share, axis=2).astype(jnp.int32)

    kv = jnp.stack([keys, values]).reshape(2, own_blocks, bt, kv_heads, HEAD_SIZE)
    kv = kv.transpose(3, 0, 1, 2, 4)
    chunk = kv_heads // CHUNKS
    windows = []
    for c in range(CHUNKS):
        mine = kv[c * chunk : (c + 1) * chunk]
        near = jnp.concatenate(
            [mine] + [rolled(mine, "head", j) for j in range(1, split)], axis=2
        )
        parts = [near]
        for _ in range(HOPS):
            parts.append(shifted(parts[-1], "ctx", 1))
        windows.append(jnp.concatenate(parts, axis=2))

    so_far = None
    grads = []
    for c in range(CHUNKS):
        attended, query_grad, part = attend(
            slot_of, spans, info, queries, out_grad, windows[c], c * chunk, so_far
        )
        so_far = (attended, query_grad)
        summed = part[:, :, HOPS * group :]
        for hop_index in range(HOPS - 1, -1, -1):
            own_part = part[:, :, hop_index * group : (hop_index + 1) * group]
            summed = (
                shifted(summed, "ctx", -1).astype(jnp.float32) + own_part.astype(jnp.float32)
            ).astype(jnp.bfloat16)
        total = summed[:, :, :own_blocks].astype(jnp.float32)
        for j in range(1, split):
            piece = summed[:, :, j * own_blocks : (j + 1) * own_blocks]
            total = total + rolled(piece, "head", -j).astype(jnp.float32)
        grads.append(total.astype(jnp.bfloat16))
    grad = jnp.concatenate(grads, axis=0).transpose(1, 2, 3, 0, 4)
    grad = grad.reshape(2, tokens, kv_heads, HEAD_SIZE)
    return so_far[0], so_far[1], grad[0], grad[1]


def solution(mesh):
    spec = P(("ctx", "head"), None, None)
    return jax.shard_map(
        body,
        mesh=mesh,
        in_specs=(spec, spec, spec, spec, P(), P()),
        out_specs=(spec, spec, spec, spec),
        check_vma=False,
    )
```

```python
import functools
import math

import jax
import jax.numpy as jnp
from jax import lax
from jax.experimental import pallas as pl
from jax.experimental.pallas import tpu as pltpu
from jax.sharding import PartitionSpec as P

HEAD_SIZE = 128
BLOCK_TOKENS = 128
HOPS = 2
DOC_MOST = 1024
CHUNKS = (2, 4, 2)
SIDE = 2
NEG_BIG = -1e30
SCALE = HEAD_SIZE ** (-0.5)
SCALE_LOG2 = SCALE * math.log2(math.e)

NN = (((1,), (0,)), ((), ()))
NT = (((1,), (1,)), ((), ()))
TN = (((0,), (0,)), ((), ()))


def dot(a, b, dims):
    return lax.dot_general(a, b, dims, preferred_element_type=jnp.float32)


def attention_kernel(slot_ref, span_ref, info_ref, q_ref, g_ref, kv_ref, *rest):
    o_ref, dq_ref, dkv_ref = rest[-3 - 5 * SIDE : -5 * SIDE]
    scratch = rest[-5 * SIDE :]
    s_scr, e_scr, out_acc, dq_acc, dkv_acc = (scratch[k * SIDE : (k + 1) * SIDE] for k in range(5))
    turn = pl.program_id(1)
    bt = q_ref.shape[0]
    share = q_ref.shape[1] // SIDE
    rows = bt * share
    sides = range(SIDE)

    @pl.when(turn == 0)
    def _():
        for a in sides:
            dkv_acc[a][...] = jnp.zeros_like(dkv_acc[a])

    last = span_ref[3 * turn]
    tiles = span_ref[3 * turn + 1]
    clean = span_ref[3 * turn + 2]
    query = [q_ref[:, a * share : (a + 1) * share, :].reshape(rows, HEAD_SIZE) for a in sides]
    query_t = [q.T for q in query]
    start = info_ref[0, 0:1, :]
    place = info_ref[0, 1:2, :]

    def slots(t):
        high = last - 2 * t
        return slot_ref[jnp.maximum(high - 1, 0)], slot_ref[high]

    def tile_of(a, which, t):
        low, high = slots(t)
        return jnp.concatenate([kv_ref[a, which, low], kv_ref[a, which, high]], axis=0)

    def fold(x, op):
        return op(x.reshape(2 * bt // 8, 8, rows), axis=0)

    def scores(t, lower, upper):
        found = []
        if lower:
            kpos = (last - 2 * t - 1) * bt + lax.broadcasted_iota(jnp.int32, (2 * bt, 1), 0)
            keep = kpos >= start
            if upper:
                keep = keep & (kpos <= place)
        for a in sides:
            s = dot(tile_of(a, 0, t), query_t[a], NN)
            if lower:
                s = jnp.where(keep, s, NEG_BIG)
            s_scr[a][t] = s
            found.append(fold(s, jnp.max))
        return found

    def larger(lower):
        return lambda t, m: [jnp.maximum(x, y) for x, y in zip(m, scores(t, lower, False))]

    best = scores(0, True, True)
    best = lax.fori_loop(1, clean, larger(False), best)
    best = lax.fori_loop(clean, tiles, larger(True), best)
    top = [jnp.max(m, axis=0, keepdims=True) * SCALE_LOG2 for m in best]

    for a in sides:
        out_acc[a][...] = jnp.zeros_like(out_acc[a])
        dq_acc[a][...] = jnp.zeros_like(dq_acc[a])

    def weights(t, totals):
        new = []
        for a in sides:
            e = jnp.exp2(s_scr[a][t] * SCALE_LOG2 - top[a])
            low = e.astype(jnp.bfloat16)
            e_scr[a][t] = low
            out_acc[a][...] += dot(tile_of(a, 1, t), low, TN)
            new.append(totals[a] + fold(e, jnp.sum))
        return new

    totals = lax.fori_loop(0, tiles, weights, [jnp.zeros((8, rows), jnp.float32)] * SIDE)
    grad_t, grad, delta = [], [], []
    for a in sides:
        inv = 1.0 / jnp.sum(totals[a], axis=0, keepdims=True)
        own = slice(a * share, (a + 1) * share)
        out_t = (out_acc[a][...] * inv).astype(jnp.bfloat16)
        o_ref[:, own, :] = out_t.T.reshape(bt, share, HEAD_SIZE)
        raw = g_ref[:, own, :].reshape(rows, HEAD_SIZE).T
        scaled = (raw.astype(jnp.float32) * inv).astype(jnp.bfloat16)
        product = scaled.astype(jnp.float32) * out_t.astype(jnp.float32)
        delta.append(jnp.sum(product, axis=0, keepdims=True))
        grad_t.append(scaled)
        grad.append(scaled.T)

    def back(t, carry):
        low, high = slots(t)
        for a in sides:
            e = e_scr[a][t]
            dp = dot(tile_of(a, 1, t), grad_t[a], NN)
            ds = (e.astype(jnp.float32) * (dp - delta[a])).astype(jnp.bfloat16)
            dq_acc[a][...] += dot(tile_of(a, 0, t), ds, TN)
            dk = dot(ds, query[a], NN)
            dv = dot(e, grad[a], NN)
            dkv_acc[a][0, low] += dk[:bt]
            dkv_acc[a][0, high] += dk[bt:]
            dkv_acc[a][1, low] += dv[:bt]
            dkv_acc[a][1, high] += dv[bt:]
        return carry

    lax.fori_loop(0, tiles, back, 0)
    for a in sides:
        own = slice(a * share, (a + 1) * share)
        dq = (dq_acc[a][...] * SCALE).astype(jnp.bfloat16)
        dq_ref[:, own, :] = dq.T.reshape(bt, share, HEAD_SIZE)

    @pl.when(turn == pl.num_programs(1) - 1)
    def _():
        for a in sides:
            dkv_ref[a, 0] = (dkv_acc[a][0] * SCALE).astype(jnp.bfloat16)
            dkv_ref[a, 1] = dkv_acc[a][1].astype(jnp.bfloat16)


def attend(slot_of, spans, info, queries, out_grad, window, first_head, so_far):
    tokens, heads, _ = queries.shape
    chunk, _, wblocks = window.shape[:3]
    bt = window.shape[3]
    share = info.shape[2] // bt
    turns = tokens // bt
    rows = bt * share
    max_tiles = DOC_MOST // bt // 2 + 1
    by_head = pl.BlockSpec(
        (bt, SIDE * share, HEAD_SIZE), lambda h, i, *_: (i, first_head // SIDE + h, 0)
    )
    kv_spec = pl.BlockSpec(
        (SIDE, 2, wblocks, bt, HEAD_SIZE), lambda h, i, *_: (h, 0, 0, 0, 0)
    )
    in_specs = [
        pl.BlockSpec((1, 2, rows), lambda h, i, *_: (i, 0, 0)),
        by_head,
        by_head,
        kv_spec,
    ]
    operands = [slot_of, spans, info, queries, out_grad, window]
    aliases = {}
    if so_far is not None:
        in_specs += [pl.BlockSpec(memory_space=pl.ANY)] * 2
        operands += list(so_far)
        aliases = {6: 0, 7: 1}
    big = jax.ShapeDtypeStruct(queries.shape, jnp.bfloat16)
    pairs = chunk * turns * rows * 6 * bt
    return pl.pallas_call(
        attention_kernel,
        grid_spec=pltpu.PrefetchScalarGridSpec(
            num_scalar_prefetch=2,
            grid=(chunk // SIDE, turns),
            in_specs=in_specs,
            out_specs=[by_head, by_head, kv_spec],
            scratch_shapes=[pltpu.VMEM((max_tiles, 2 * bt, rows), jnp.float32)] * SIDE
            + [pltpu.VMEM((max_tiles, 2 * bt, rows), jnp.bfloat16)] * SIDE
            + [pltpu.VMEM((HEAD_SIZE, rows), jnp.float32)] * (2 * SIDE)
            + [pltpu.VMEM((2, wblocks, bt, HEAD_SIZE), jnp.float32)] * SIDE,
        ),
        out_shape=[big, big, jax.ShapeDtypeStruct(window.shape, jnp.bfloat16)],
        input_output_aliases=aliases,
        compiler_params=pltpu.CompilerParams(vmem_limit_bytes=48 * 1024 * 1024),
        cost_estimate=pl.CostEstimate(
            flops=12 * pairs * HEAD_SIZE,
            bytes_accessed=4 * chunk * tokens * share * HEAD_SIZE * 2 + 4 * window.size,
            transcendentals=pairs,
        ),
    )(*operands)


def shifted(block, axis, distance):
    size = lax.axis_size(axis)
    route = [(i - distance, i) for i in range(size) if 0 <= i - distance < size]
    return lax.ppermute(block, axis, route)


def rolled(block, axis, distance):
    size = lax.axis_size(axis)
    return lax.ppermute(block, axis, [(i, (i + distance) % size) for i in range(size)])


def body(queries, keys, values, out_grad, doc_lengths, stored_block_order):
    tokens, heads, _ = queries.shape
    bt = min(BLOCK_TOKENS, tokens)
    pieces = BLOCK_TOKENS // bt
    stored_order = stored_block_order[:, None] * pieces + jnp.arange(pieces, dtype=jnp.int32)
    stored_order = stored_order.reshape(-1)
    kv_heads = keys.shape[1]
    share = heads // kv_heads
    own_blocks = tokens // bt
    split = lax.axis_size("head")
    me_head, me_ctx = lax.axis_index("head"), lax.axis_index("ctx")
    group = own_blocks * split
    window_blocks = (HOPS + 1) * group

    w = jnp.arange(window_blocks, dtype=jnp.int32)
    hop, turn, inner = w // group, (w % group) // own_blocks, w % own_blocks
    source = lax.rem(me_head - turn + split, split)
    stored = jnp.maximum(me_ctx - hop, 0) * group + source * own_blocks + inner
    rel = (HOPS - hop) * group + stored_order[stored] % group
    slot_of = jnp.sum(jnp.where(rel[None, :] == w[:, None], w[None, :], 0), axis=1).astype(jnp.int32)

    own = (me_ctx * split + me_head) * own_blocks
    base = (me_ctx - HOPS) * group
    blocks = lax.dynamic_slice_in_dim(stored_order, own, own_blocks, 0) - base
    place = blocks[:, None] * bt + jnp.arange(bt, dtype=jnp.int32)[None, :]
    ends = jnp.cumsum(doc_lengths).astype(jnp.int32) - base * bt
    start = jnp.max(
        jnp.where(ends[None, None, :] <= place[..., None], ends[None, None, :], -base * bt), axis=-1
    )
    tiles = (blocks - start[:, 0] // bt) // 2 + 1
    clean = (blocks - 1 + (-start[:, -1]) // bt) // 2 + 1
    clean = jnp.clip(clean, 1, tiles)
    spans = jnp.stack([blocks, tiles, clean], axis=1).reshape(-1).astype(jnp.int32)
    info = jnp.repeat(jnp.stack([start, place], axis=1), share, axis=2).astype(jnp.int32)

    kv = jnp.stack([keys, values]).reshape(2, own_blocks, bt, kv_heads, HEAD_SIZE)
    kv = kv.transpose(3, 0, 1, 2, 4)
    firsts = [sum(CHUNKS[:c]) for c in range(len(CHUNKS))]

    def with_others(part):
        return jnp.concatenate([part] + [rolled(part, "head", j) for j in range(1, split)], axis=2)

    near_first = with_others(kv[: CHUNKS[0]])
    near_rest = with_others(kv[CHUNKS[0] :])
    windows = []
    for first, chunk in zip(firsts, CHUNKS):
        if first == 0:
            near = near_first
        else:
            near = near_rest[first - CHUNKS[0] : first - CHUNKS[0] + chunk]
        far = [shifted(near, "ctx", hop_index) for hop_index in range(1, HOPS + 1)]
        windows.append(jnp.concatenate([near] + far, axis=2))

    so_far = None
    sums = []
    for first, window in zip(firsts, windows):
        attended, query_grad, part = attend(
            slot_of, spans, info, queries, out_grad, window, first, so_far
        )
        so_far = (attended, query_grad)
        summed = part[:, :, :group].astype(jnp.float32)
        for hop_index in range(1, HOPS + 1):
            piece = part[:, :, hop_index * group : (hop_index + 1) * group]
            summed = summed + shifted(piece, "ctx", -hop_index).astype(jnp.float32)
        sums.append(summed.astype(jnp.bfloat16))

    def over_heads(summed):
        total = summed[:, :, :own_blocks].astype(jnp.float32)
        for j in range(1, split):
            piece = summed[:, :, j * own_blocks : (j + 1) * own_blocks]
            total = total + rolled(piece, "head", -j).astype(jnp.float32)
        return total.astype(jnp.bfloat16)

    grads = [over_heads(jnp.concatenate(sums[:-1], axis=0)), over_heads(sums[-1])]
    grad = jnp.concatenate(grads, axis=0).transpose(1, 2, 3, 0, 4)
    grad = grad.reshape(2, tokens, kv_heads, HEAD_SIZE)
    return so_far[0], so_far[1], grad[0], grad[1]


def solution(mesh):
    spec = P(("ctx", "head"), None, None)
    return jax.shard_map(
        body,
        mesh=mesh,
        in_specs=(spec, spec, spec, spec, P(), P()),
        out_specs=(spec, spec, spec, spec),
        check_vma=False,
    )
```

```python
import functools
import math

import jax
import jax.numpy as jnp
from jax import lax
from jax.experimental import pallas as pl
from jax.experimental.pallas import tpu as pltpu
from jax.sharding import PartitionSpec as P

HEAD_SIZE = 128
BLOCK_TOKENS = 128
HOPS = 2
DOC_MOST = 1024
SIDE = 2
NEG_BIG = -1e30
SCALE = HEAD_SIZE ** (-0.5)
SCALE_LOG2 = SCALE * math.log2(math.e)

NN = (((1,), (0,)), ((), ()))
NT = (((1,), (1,)), ((), ()))
TN = (((0,), (0,)), ((), ()))


def dot(a, b, dims):
    return lax.dot_general(a, b, dims, preferred_element_type=jnp.float32)


def fused_kernel(tab_ref, inv_ref, info_ref, q_ref, g_ref, kv_ref, o_ref, dq_ref, dkv_ref, *scratch):
    s_scr, e_scr, out_acc, dq_acc, part, acc = (scratch[k * SIDE : (k + 1) * SIDE] for k in range(6))
    near, land, stage, back_land, own, send, recv, back_send, back_recv = scratch[6 * SIDE :]
    step, turn = pl.program_id(0), pl.program_id(1)
    steps, turns = pl.num_programs(0), pl.num_programs(1)
    bt = q_ref.shape[0]
    share = q_ref.shape[1] // SIDE
    rows = bt * share
    sides = range(SIDE)
    max_tiles = s_scr[0].shape[0]
    reach = 2 * max_tiles
    own_blocks = kv_ref.shape[3]
    split, row = lax.axis_size("head"), lax.axis_size("ctx")
    me_head, me_ctx = lax.axis_index("head"), lax.axis_index("ctx")
    groups = (HOPS + 1) * split
    window_blocks = groups * own_blocks

    def ahead(g):
        return {"ctx": lax.rem(me_ctx + g // split, row), "head": lax.rem(me_head + g % split, split)}

    def behind(g):
        return {
            "ctx": lax.rem(me_ctx + row - g // split, row),
            "head": lax.rem(me_head + split - g % split, split),
        }

    def has_ahead(g):
        return me_ctx + g // split < row

    def has_behind(g):
        return me_ctx >= g // split

    def forth(g, p):
        return pltpu.make_async_remote_copy(
            src_ref=kv_ref.at[p], dst_ref=land.at[p, g - 1],
            send_sem=send.at[p, g - 1], recv_sem=recv.at[p, g - 1],
            device_id=ahead(g), device_id_type=pl.DeviceIdType.MESH,
        )

    def home(g, p):
        return pltpu.make_async_remote_copy(
            src_ref=stage.at[p, g - 1], dst_ref=back_land.at[p, g - 1],
            send_sem=back_send.at[p, g - 1], recv_sem=back_recv.at[p, g - 1],
            device_id=behind(g), device_id_type=pl.DeviceIdType.MESH,
        )

    def send_forth(p):
        for g in range(1, groups):
            @pl.when(has_ahead(g))
            def _():
                forth(g, p).start()

    @pl.when((step == 0) & (turn == 0))
    def _():
        barrier = pltpu.get_barrier_semaphore()
        for g in range(1, groups):
            @pl.when(has_ahead(g))
            def _():
                pl.semaphore_signal(
                    barrier, inc=1, device_id=ahead(g), device_id_type=pl.DeviceIdType.MESH
                )

            if g >= split:
                @pl.when(has_behind(g))
                def _():
                    pl.semaphore_signal(
                        barrier, inc=1, device_id=behind(g), device_id_type=pl.DeviceIdType.MESH
                    )

        peers = split - 1
        for d in range(1, HOPS + 1):
            ends = (me_ctx + d < row).astype(jnp.int32) + (me_ctx >= d).astype(jnp.int32)
            peers = peers + split * ends
        pl.semaphore_wait(barrier, peers)

        send_forth(0)
        for a in sides:
            part[a][:, reach] = jnp.zeros((2, bt, HEAD_SIZE), jnp.float32)

    @pl.when(turn == 0)
    def _():
        for a in sides:
            near[a, :, :own_blocks] = kv_ref[step, a]
        for g in range(1, groups):
            place_of = slice(g * own_blocks, (g + 1) * own_blocks)

            @pl.when(has_behind(g))
            def _():
                forth(g, step).wait_recv()
                near[:, :, place_of] = land[step, g - 1]

            @pl.when(jnp.logical_not(has_behind(g)))
            def _():
                near[:, :, place_of] = jnp.zeros((SIDE, 2, own_blocks, bt, HEAD_SIZE), jnp.bfloat16)

        @pl.when(step + 1 < steps)
        def _():
            send_forth(step + 1)

    query = [q_ref[:, a * share : (a + 1) * share, :].reshape(rows, HEAD_SIZE) for a in sides]
    query_t = [q.T for q in query]
    start = info_ref[turn, 0:1, :]
    place = info_ref[turn, 1:2, :]

    def tile_of(a, which, t):
        low = tab_ref[turn * reach + 2 * t + 1]
        high = tab_ref[turn * reach + 2 * t]
        return jnp.concatenate([near[a, which, low], near[a, which, high]], axis=0)

    def fold(x, op):
        return op(x.reshape(2 * bt // 8, 8, rows), axis=0)

    def scores(t, upper):
        found = []
        kpos = lax.broadcasted_iota(jnp.int32, (2 * bt, 1), 0) - (2 * t + 1) * bt
        keep = kpos >= start
        if upper:
            keep = keep & (kpos <= place)
        for a in sides:
            s = dot(tile_of(a, 0, t), query_t[a], NN)
            s = jnp.where(keep, s, NEG_BIG)
            s_scr[a][t] = s
            found.append(fold(s, jnp.max))
        return found

    best = scores(0, True)
    best = lax.fori_loop(
        1, max_tiles, lambda t, m: [jnp.maximum(x, y) for x, y in zip(m, scores(t, False))], best
    )
    top = [jnp.max(m, axis=0, keepdims=True) * SCALE_LOG2 for m in best]

    for a in sides:
        out_acc[a][...] = jnp.zeros_like(out_acc[a])
        dq_acc[a][...] = jnp.zeros_like(dq_acc[a])

    def weights(t, totals):
        new = []
        for a in sides:
            e = jnp.exp2(s_scr[a][t] * SCALE_LOG2 - top[a])
            low = e.astype(jnp.bfloat16)
            e_scr[a][t] = low
            out_acc[a][...] += dot(tile_of(a, 1, t), low, TN)
            new.append(totals[a] + fold(e, jnp.sum))
        return new

    totals = lax.fori_loop(0, max_tiles, weights, [jnp.zeros((8, rows), jnp.float32)] * SIDE)
    grad_t, grad, delta = [], [], []
    for a in sides:
        inv = 1.0 / jnp.sum(totals[a], axis=0, keepdims=True)
        mine = slice(a * share, (a + 1) * share)
        out_t = (out_acc[a][...] * inv).astype(jnp.bfloat16)
        o_ref[:, mine, :] = out_t.T.reshape(bt, share, HEAD_SIZE)
        raw = g_ref[:, mine, :].reshape(rows, HEAD_SIZE).T
        scaled = (raw.astype(jnp.float32) * inv).astype(jnp.bfloat16)
        product = scaled.astype(jnp.float32) * out_t.astype(jnp.float32)
        delta.append(jnp.sum(product, axis=0, keepdims=True))
        grad_t.append(scaled)
        grad.append(scaled.T)

    def back(t, carry):
        for a in sides:
            e = e_scr[a][t]
            dp = dot(tile_of(a, 1, t), grad_t[a], NN)
            ds = (e.astype(jnp.float32) * (dp - delta[a])).astype(jnp.bfloat16)
            dq_acc[a][...] += dot(tile_of(a, 0, t), ds, TN)
            dk = dot(ds, query[a], NN)
            dv = dot(e, grad[a], NN)
            part[a][0, 2 * t + 1] = dk[:bt]
            part[a][0, 2 * t] = dk[bt:]
            part[a][1, 2 * t + 1] = dv[:bt]
            part[a][1, 2 * t] = dv[bt:]
        return carry

    lax.fori_loop(0, max_tiles, back, 0)
    for a in sides:
        mine = slice(a * share, (a + 1) * share)
        dq = (dq_acc[a][...] * SCALE).astype(jnp.bfloat16)
        dq_ref[:, mine, :] = dq.T.reshape(bt, share, HEAD_SIZE)

    @pl.when(turn == 0)
    def _():
        for a in sides:
            acc[a][...] = jnp.zeros_like(acc[a])

    for w in range(window_blocks):
        found = inv_ref[turn * window_blocks + w]
        for a in sides:
            for which in range(2):
                acc[a][which, w] += part[a][which, found]

    def finish(p):
        for g in range(1, groups):
            @pl.when(has_ahead(g))
            def _():
                home(g, p).wait_recv()
                own[p] += back_land[p, g - 1].astype(jnp.float32)
        for a in sides:
            dkv_ref[p * SIDE + a] = own[p, a].astype(jnp.bfloat16)

    @pl.when(turn == turns - 1)
    def _():
        for a in sides:
            for which in range(2):
                factor = SCALE if which == 0 else 1.0
                for g in range(1, groups):
                    piece = acc[a][which, g * own_blocks : (g + 1) * own_blocks] * factor
                    stage[step, g - 1, a, which] = piece.astype(jnp.bfloat16)
                own[step, a, which] = acc[a][which, :own_blocks] * factor
        for g in range(1, groups):
            @pl.when(has_behind(g))
            def _():
                home(g, step).start()

        @pl.when(step > 0)
        def _():
            finish(step - 1)

        @pl.when(step == steps - 1)
        def _():
            finish(step)
            for p in range(send.shape[0]):
                for g in range(1, groups):
                    @pl.when(has_ahead(g))
                    def _():
                        forth(g, p).wait_send()

                    @pl.when(has_behind(g))
                    def _():
                        home(g, p).wait_send()


def attend(table, inverse, info, queries, out_grad, kv, split):
    tokens, heads, _ = queries.shape
    steps, _, _, own_blocks, bt, _ = kv.shape
    turns = own_blocks
    rows = info.shape[2]
    share = rows // bt
    max_tiles = DOC_MOST // bt // 2 + 1
    reach = 2 * max_tiles
    groups = (HOPS + 1) * split
    window_blocks = groups * own_blocks
    by_head = pl.BlockSpec((bt, SIDE * share, HEAD_SIZE), lambda p, i: (i, p, 0))
    whole = pl.BlockSpec(memory_space=pltpu.VMEM)
    table_spec = pl.BlockSpec(memory_space=pltpu.SMEM)
    big = jax.ShapeDtypeStruct(queries.shape, jnp.bfloat16)
    pairs = steps * SIDE * turns * rows * reach * bt
    f32, low = jnp.float32, jnp.bfloat16
    piece = (SIDE, 2, own_blocks, bt, HEAD_SIZE)
    far = (steps, groups - 1) + piece
    sems = pltpu.SemaphoreType.DMA((steps, groups - 1))
    return pl.pallas_call(
        fused_kernel,
        grid=(steps, turns),
        in_specs=[table_spec, table_spec, whole, by_head, by_head, whole],
        out_specs=[by_head, by_head, whole],
        scratch_shapes=[pltpu.VMEM((max_tiles, 2 * bt, rows), f32)] * SIDE
        + [pltpu.VMEM((max_tiles, 2 * bt, rows), low)] * SIDE
        + [pltpu.VMEM((HEAD_SIZE, rows), f32)] * (2 * SIDE)
        + [pltpu.VMEM((2, reach + 1, bt, HEAD_SIZE), f32)] * SIDE
        + [pltpu.VMEM((2, window_blocks, bt, HEAD_SIZE), f32)] * SIDE
        + [
            pltpu.VMEM((SIDE, 2, window_blocks, bt, HEAD_SIZE), low),
            pltpu.VMEM(far, low),
            pltpu.VMEM(far, low),
            pltpu.VMEM(far, low),
            pltpu.VMEM((steps,) + piece, f32),
            sems,
            sems,
            sems,
            sems,
        ],
        out_shape=[big, big, jax.ShapeDtypeStruct((steps * SIDE,) + piece[1:], low)],
        compiler_params=pltpu.CompilerParams(
            collective_id=0, has_side_effects=True, vmem_limit_bytes=60 * 1024 * 1024
        ),
        cost_estimate=pl.CostEstimate(
            flops=12 * pairs * HEAD_SIZE,
            bytes_accessed=4 * queries.size * 2,
            transcendentals=pairs,
        ),
    )(table, inverse, info, queries, out_grad, kv)


def body(queries, keys, values, out_grad, doc_lengths, stored_block_order):
    tokens, heads, _ = queries.shape
    bt = min(BLOCK_TOKENS, tokens)
    pieces = BLOCK_TOKENS // bt
    stored_order = stored_block_order[:, None] * pieces + jnp.arange(pieces, dtype=jnp.int32)
    stored_order = stored_order.reshape(-1)
    kv_heads = keys.shape[1]
    share = heads // kv_heads
    own_blocks = tokens // bt
    split = lax.axis_size("head")
    me_head, me_ctx = lax.axis_index("head"), lax.axis_index("ctx")
    group = own_blocks * split
    window_blocks = (HOPS + 1) * group

    w = jnp.arange(window_blocks, dtype=jnp.int32)
    hop, turn, inner = w // group, (w % group) // own_blocks, w % own_blocks
    source = lax.rem(me_head - turn + split, split)
    stored = jnp.maximum(me_ctx - hop, 0) * group + source * own_blocks + inner
    rel = (HOPS - hop) * group + stored_order[stored] % group
    slot_of = jnp.sum(jnp.where(rel[None, :] == w[:, None], w[None, :], 0), axis=1).astype(jnp.int32)

    own = (me_ctx * split + me_head) * own_blocks
    base = (me_ctx - HOPS) * group
    blocks = lax.dynamic_slice_in_dim(stored_order, own, own_blocks, 0) - base
    place = blocks[:, None] * bt + jnp.arange(bt, dtype=jnp.int32)[None, :]
    ends = jnp.cumsum(doc_lengths).astype(jnp.int32) - base * bt
    start = jnp.max(
        jnp.where(ends[None, None, :] <= place[..., None], ends[None, None, :], -base * bt), axis=-1
    )
    reach = 2 * (DOC_MOST // bt // 2 + 1)
    back = blocks[:, None] - jnp.arange(reach, dtype=jnp.int32)[None, :]
    table = slot_of[jnp.maximum(back, 0)].reshape(-1)
    gap = blocks[:, None] - rel[None, :]
    inverse = jnp.where((gap >= 0) & (gap < reach), gap, reach).reshape(-1).astype(jnp.int32)
    first = blocks[:, None] * bt
    info = jnp.stack([start - first, place - first], axis=1)
    info = jnp.repeat(info, share, axis=2).astype(jnp.int32)

    kv = jnp.stack([keys, values]).reshape(2, own_blocks, bt, kv_heads, HEAD_SIZE)
    kv = kv.transpose(3, 0, 1, 2, 4)
    kv = kv.reshape(kv_heads // SIDE, SIDE, 2, own_blocks, bt, HEAD_SIZE)
    attended, query_grad, grad = attend(table, inverse, info, queries, out_grad, kv, split)
    grad = grad.transpose(1, 2, 3, 0, 4).reshape(2, tokens, kv_heads, HEAD_SIZE)
    return attended, query_grad, grad[0], grad[1]


def solution(mesh):
    spec = P(("ctx", "head"), None, None)
    return jax.shard_map(
        body,
        mesh=mesh,
        in_specs=(spec, spec, spec, spec, P(), P()),
        out_specs=(spec, spec, spec, spec),
        check_vma=False,
    )
```

```python
import functools
import math

import jax
import jax.numpy as jnp
from jax import lax
from jax.experimental import pallas as pl
from jax.experimental.pallas import tpu as pltpu
from jax.sharding import PartitionSpec as P

HEAD_SIZE = 128
BLOCK_TOKENS = 128
HOPS = 2
DOC_MOST = 1024
SIDE = 2
NEG_BIG = -1e30
SCALE = HEAD_SIZE ** (-0.5)
SCALE_LOG2 = SCALE * math.log2(math.e)

NN = (((1,), (0,)), ((), ()))
NT = (((1,), (1,)), ((), ()))
TN = (((0,), (0,)), ((), ()))


def dot(a, b, dims):
    return lax.dot_general(a, b, dims, preferred_element_type=jnp.float32)


def fused_kernel(tab_ref, inv_ref, info_ref, q_ref, g_ref, kv_ref, o_ref, dq_ref, dkv_ref, *scratch):
    s_scr, e_scr, out_acc, dq_acc, part, acc = (scratch[k * SIDE : (k + 1) * SIDE] for k in range(6))
    near, land, stage, back_land, mate_land, own = scratch[6 * SIDE : 6 * SIDE + 6]
    send, recv, pass_send, back_send, back_recv, mate_send, mate_recv = scratch[6 * SIDE + 6 :]
    step, turn = pl.program_id(0), pl.program_id(1)
    steps, turns = pl.num_programs(0), pl.num_programs(1)
    bt = q_ref.shape[0]
    share = q_ref.shape[1] // SIDE
    rows = bt * share
    sides = range(SIDE)
    max_tiles = s_scr[0].shape[0]
    reach = 2 * max_tiles
    own_blocks = kv_ref.shape[3]
    split, row = lax.axis_size("head"), lax.axis_size("ctx")
    me_head, me_ctx = lax.axis_index("head"), lax.axis_index("ctx")
    groups = (HOPS + 1) * split
    window_blocks = groups * own_blocks
    even = lax.rem(me_ctx, 2) == 0
    odd = jnp.logical_not(even)
    mesh_ids = pl.DeviceIdType.MESH

    def ahead(g):
        return {"ctx": lax.rem(me_ctx + g // split, row), "head": lax.rem(me_head + g % split, split)}

    def behind(g):
        return {
            "ctx": lax.rem(me_ctx + row - g // split, row),
            "head": lax.rem(me_head + split - g % split, split),
        }

    def has_ahead(g):
        return me_ctx + g // split < row

    def has_behind(g):
        return me_ctx >= g // split

    def forth(g, p):
        return pltpu.make_async_remote_copy(
            src_ref=kv_ref.at[p], dst_ref=land.at[p, g - 1],
            send_sem=send.at[p, g - 1], recv_sem=recv.at[p, g - 1],
            device_id=ahead(g), device_id_type=pl.DeviceIdType.MESH,
        )

    def home(g, p):
        return pltpu.make_async_remote_copy(
            src_ref=stage.at[p, g - 1], dst_ref=back_land.at[p, g - 1],
            send_sem=back_send.at[p, g - 1], recv_sem=back_recv.at[p, g - 1],
            device_id=behind(g), device_id_type=pl.DeviceIdType.MESH,
        )

    def passed(g, p):
        source = kv_ref.at[p] if g == split else land.at[p, g - split - 1]
        return pltpu.make_async_remote_copy(
            src_ref=source, dst_ref=land.at[p, g - 1],
            send_sem=pass_send.at[p, g - 1], recv_sem=recv.at[p, g - 1],
            device_id={"ctx": lax.rem(me_ctx + 1, row), "head": me_head}, device_id_type=mesh_ids,
        )

    def to_mate(g, p):
        return pltpu.make_async_remote_copy(
            src_ref=stage.at[p, g - 1], dst_ref=mate_land.at[p, g - 1],
            send_sem=mate_send.at[p, g - 1], recv_sem=mate_recv.at[p, g - 1],
            device_id={"ctx": lax.rem(me_ctx + row - 1, row), "head": me_head},
            device_id_type=mesh_ids,
        )

    def sends_forth(g):
        return has_ahead(g) if g < split else has_ahead(g) & (lax.rem(me_ctx + g // split, 2) == 0)

    def sends_home(g):
        return has_behind(g) if g < split else has_behind(g) & even

    def passes(g):
        return even & has_behind(g - split)

    def send_forth(p):
        for g in range(1, groups):
            @pl.when(sends_forth(g))
            def _():
                forth(g, p).start()

        @pl.when(even)
        def _():
            passed(split, p).start()

    def arrive(p):
        for g in range(1, groups):
            @pl.when(has_behind(g))
            def _():
                forth(g, p).wait_recv()

    def pass_on(p):
        @pl.when(even)
        def _():
            arrive(p)
        for g in range(split + 1, groups):
            @pl.when(passes(g))
            def _():
                passed(g, p).start()

    def settle(p):
        for g in range(groups - split):
            @pl.when(even & has_behind(g))
            def _():
                to_mate(g + split, p).wait_recv()
                other = mate_land[p, g + split - 1].astype(jnp.float32)
                if g == 0:
                    own[p] += other
                else:
                    stage[p, g - 1] = (stage[p, g - 1].astype(jnp.float32) + other).astype(
                        jnp.bfloat16
                    )
                    home(g, p).start()

    @pl.when((step == 0) & (turn == 0))
    def _():
        barrier = pltpu.get_barrier_semaphore()
        for g in range(1, groups):
            @pl.when(has_ahead(g))
            def _():
                pl.semaphore_signal(
                    barrier, inc=1, device_id=ahead(g), device_id_type=pl.DeviceIdType.MESH
                )

            if g >= split:
                @pl.when(has_behind(g))
                def _():
                    pl.semaphore_signal(
                        barrier, inc=1, device_id=behind(g), device_id_type=pl.DeviceIdType.MESH
                    )

        peers = split - 1
        for d in range(1, HOPS + 1):
            ends = (me_ctx + d < row).astype(jnp.int32) + (me_ctx >= d).astype(jnp.int32)
            peers = peers + split * ends
        pl.semaphore_wait(barrier, peers)

        send_forth(0)
        pass_on(0)
        for a in sides:
            part[a][:, reach] = jnp.zeros((2, bt, HEAD_SIZE), jnp.float32)

    @pl.when(turn == 0)
    def _():
        @pl.when(odd)
        def _():
            arrive(step)
        for a in sides:
            near[a, :, :own_blocks] = kv_ref[step, a]
        for g in range(1, groups):
            place_of = slice(g * own_blocks, (g + 1) * own_blocks)

            @pl.when(has_behind(g))
            def _():
                near[:, :, place_of] = land[step, g - 1]

            @pl.when(jnp.logical_not(has_behind(g)))
            def _():
                near[:, :, place_of] = jnp.zeros((SIDE, 2, own_blocks, bt, HEAD_SIZE), jnp.bfloat16)

        @pl.when(step == 0)
        def _():
            send_forth(1)

    @pl.when(turn == turns - 1)
    def _():
        @pl.when(step + 1 < steps)
        def _():
            pass_on(step + 1)

        @pl.when(step + 2 < steps)
        def _():
            send_forth(step + 2)

        @pl.when(step > 0)
        def _():
            settle(step - 1)

    query = [q_ref[:, a * share : (a + 1) * share, :].reshape(rows, HEAD_SIZE) for a in sides]
    query_t = [q.T for q in query]
    start = info_ref[turn, 0:1, :]
    place = info_ref[turn, 1:2, :]

    def tile_of(a, which, t):
        low = tab_ref[turn * reach + 2 * t + 1]
        high = tab_ref[turn * reach + 2 * t]
        return jnp.concatenate([near[a, which, low], near[a, which, high]], axis=0)

    def fold(x, op):
        return op(x.reshape(2 * bt // 8, 8, rows), axis=0)

    def scores(t, upper):
        found = []
        kpos = lax.broadcasted_iota(jnp.int32, (2 * bt, 1), 0) - (2 * t + 1) * bt
        keep = kpos >= start
        if upper:
            keep = keep & (kpos <= place)
        for a in sides:
            s = dot(tile_of(a, 0, t), query_t[a], NN)
            s = jnp.where(keep, s, NEG_BIG)
            s_scr[a][t] = s
            found.append(fold(s, jnp.max))
        return found

    best = scores(0, True)
    best = lax.fori_loop(
        1, max_tiles, lambda t, m: [jnp.maximum(x, y) for x, y in zip(m, scores(t, False))], best
    )
    top = [jnp.max(m, axis=0, keepdims=True) * SCALE_LOG2 for m in best]

    for a in sides:
        out_acc[a][...] = jnp.zeros_like(out_acc[a])
        dq_acc[a][...] = jnp.zeros_like(dq_acc[a])

    def weights(t, totals):
        new = []
        for a in sides:
            e = jnp.exp2(s_scr[a][t] * SCALE_LOG2 - top[a])
            low = e.astype(jnp.bfloat16)
            e_scr[a][t] = low
            out_acc[a][...] += dot(tile_of(a, 1, t), low, TN)
            new.append(totals[a] + fold(e, jnp.sum))
        return new

    totals = lax.fori_loop(0, max_tiles, weights, [jnp.zeros((8, rows), jnp.float32)] * SIDE)
    grad_t, grad, delta = [], [], []
    for a in sides:
        inv = 1.0 / jnp.sum(totals[a], axis=0, keepdims=True)
        mine = slice(a * share, (a + 1) * share)
        out_t = (out_acc[a][...] * inv).astype(jnp.bfloat16)
        o_ref[:, mine, :] = out_t.T.reshape(bt, share, HEAD_SIZE)
        raw = g_ref[:, mine, :].reshape(rows, HEAD_SIZE).T
        scaled = (raw.astype(jnp.float32) * inv).astype(jnp.bfloat16)
        product = scaled.astype(jnp.float32) * out_t.astype(jnp.float32)
        delta.append(jnp.sum(product, axis=0, keepdims=True))
        grad_t.append(scaled)
        grad.append(scaled.T)

    def back(t, carry):
        for a in sides:
            e = e_scr[a][t]
            dp = dot(tile_of(a, 1, t), grad_t[a], NN)
            ds = (e.astype(jnp.float32) * (dp - delta[a])).astype(jnp.bfloat16)
            dq_acc[a][...] += dot(tile_of(a, 0, t), ds, TN)
            dk = dot(ds, query[a], NN)
            dv = dot(e, grad[a], NN)
            part[a][0, 2 * t + 1] = dk[:bt]
            part[a][0, 2 * t] = dk[bt:]
            part[a][1, 2 * t + 1] = dv[:bt]
            part[a][1, 2 * t] = dv[bt:]
        return carry

    lax.fori_loop(0, max_tiles, back, 0)
    for a in sides:
        mine = slice(a * share, (a + 1) * share)
        dq = (dq_acc[a][...] * SCALE).astype(jnp.bfloat16)
        dq_ref[:, mine, :] = dq.T.reshape(bt, share, HEAD_SIZE)

    @pl.when(turn == 0)
    def _():
        for a in sides:
            acc[a][...] = jnp.zeros_like(acc[a])

    for w in range(window_blocks):
        found = inv_ref[turn * window_blocks + w]
        for a in sides:
            for which in range(2):
                acc[a][which, w] += part[a][which, found]

    def finish(p):
        for g in range(1, groups):
            comes = has_ahead(g)
            if g >= split:
                comes = comes & (lax.rem(me_ctx + g // split, 2) == 0)

            @pl.when(comes)
            def _():
                home(g, p).wait_recv()
                own[p] += back_land[p, g - 1].astype(jnp.float32)
        for a in sides:
            dkv_ref[p * SIDE + a] = own[p, a].astype(jnp.bfloat16)

    @pl.when(turn == turns - 1)
    def _():
        for a in sides:
            for which in range(2):
                factor = SCALE if which == 0 else 1.0
                for g in range(1, groups):
                    piece = acc[a][which, g * own_blocks : (g + 1) * own_blocks] * factor
                    stage[step, g - 1, a, which] = piece.astype(jnp.bfloat16)
                own[step, a, which] = acc[a][which, :own_blocks] * factor
        for g in range(1, groups):
            if g >= split:
                @pl.when(odd & has_behind(g))
                def _():
                    to_mate(g, step).start()

            @pl.when((even if g >= groups - split else odd) & sends_home(g))
            def _():
                home(g, step).start()

        @pl.when(step > 1)
        def _():
            finish(step - 2)

        @pl.when(step == steps - 1)
        def _():
            settle(step)
            finish(step - 1)
            finish(step)
            for p in range(send.shape[0]):
                for g in range(1, groups):
                    @pl.when(sends_forth(g))
                    def _():
                        forth(g, p).wait_send()

                    @pl.when(sends_home(g))
                    def _():
                        home(g, p).wait_send()

                    if g >= split:
                        @pl.when(passes(g))
                        def _():
                            passed(g, p).wait_send()

                        @pl.when(odd & has_behind(g))
                        def _():
                            to_mate(g, p).wait_send()


def attend(table, inverse, info, queries, out_grad, kv, split):
    tokens, heads, _ = queries.shape
    steps, _, _, own_blocks, bt, _ = kv.shape
    turns = own_blocks
    rows = info.shape[2]
    share = rows // bt
    max_tiles = DOC_MOST // bt // 2 + 1
    reach = 2 * max_tiles
    groups = (HOPS + 1) * split
    window_blocks = groups * own_blocks
    by_head = pl.BlockSpec((bt, SIDE * share, HEAD_SIZE), lambda p, i: (i, p, 0))
    whole = pl.BlockSpec(memory_space=pltpu.VMEM)
    table_spec = pl.BlockSpec(memory_space=pltpu.SMEM)
    big = jax.ShapeDtypeStruct(queries.shape, jnp.bfloat16)
    pairs = steps * SIDE * turns * rows * reach * bt
    f32, low = jnp.float32, jnp.bfloat16
    piece = (SIDE, 2, own_blocks, bt, HEAD_SIZE)
    far = (steps, groups - 1) + piece
    sems = pltpu.SemaphoreType.DMA((steps, groups - 1))
    return pl.pallas_call(
        fused_kernel,
        grid=(steps, turns),
        in_specs=[table_spec, table_spec, whole, by_head, by_head, whole],
        out_specs=[by_head, by_head, whole],
        scratch_shapes=[pltpu.VMEM((max_tiles, 2 * bt, rows), f32)] * SIDE
        + [pltpu.VMEM((max_tiles, 2 * bt, rows), low)] * SIDE
        + [pltpu.VMEM((HEAD_SIZE, rows), f32)] * (2 * SIDE)
        + [pltpu.VMEM((2, reach + 1, bt, HEAD_SIZE), f32)] * SIDE
        + [pltpu.VMEM((2, window_blocks, bt, HEAD_SIZE), f32)] * SIDE
        + [
            pltpu.VMEM((SIDE, 2, window_blocks, bt, HEAD_SIZE), low),
            pltpu.VMEM(far, low),
            pltpu.VMEM(far, low),
            pltpu.VMEM(far, low),
            pltpu.VMEM(far, low),
            pltpu.VMEM((steps,) + piece, f32),
            sems,
            sems,
            sems,
            sems,
            sems,
            sems,
            sems,
        ],
        out_shape=[big, big, jax.ShapeDtypeStruct((steps * SIDE,) + piece[1:], low)],
        compiler_params=pltpu.CompilerParams(
            collective_id=0, has_side_effects=True, vmem_limit_bytes=60 * 1024 * 1024
        ),
        cost_estimate=pl.CostEstimate(
            flops=12 * pairs * HEAD_SIZE,
            bytes_accessed=4 * queries.size * 2,
            transcendentals=pairs,
        ),
    )(table, inverse, info, queries, out_grad, kv)


def body(queries, keys, values, out_grad, doc_lengths, stored_block_order):
    tokens, heads, _ = queries.shape
    bt = min(BLOCK_TOKENS, tokens)
    pieces = BLOCK_TOKENS // bt
    stored_order = stored_block_order[:, None] * pieces + jnp.arange(pieces, dtype=jnp.int32)
    stored_order = stored_order.reshape(-1)
    kv_heads = keys.shape[1]
    share = heads // kv_heads
    own_blocks = tokens // bt
    split = lax.axis_size("head")
    me_head, me_ctx = lax.axis_index("head"), lax.axis_index("ctx")
    group = own_blocks * split
    window_blocks = (HOPS + 1) * group

    w = jnp.arange(window_blocks, dtype=jnp.int32)
    hop, turn, inner = w // group, (w % group) // own_blocks, w % own_blocks
    source = lax.rem(me_head - turn + split, split)
    stored = jnp.maximum(me_ctx - hop, 0) * group + source * own_blocks + inner
    rel = (HOPS - hop) * group + stored_order[stored] % group
    slot_of = jnp.sum(jnp.where(rel[None, :] == w[:, None], w[None, :], 0), axis=1).astype(jnp.int32)

    own = (me_ctx * split + me_head) * own_blocks
    base = (me_ctx - HOPS) * group
    blocks = lax.dynamic_slice_in_dim(stored_order, own, own_blocks, 0) - base
    place = blocks[:, None] * bt + jnp.arange(bt, dtype=jnp.int32)[None, :]
    ends = jnp.cumsum(doc_lengths).astype(jnp.int32) - base * bt
    start = jnp.max(
        jnp.where(ends[None, None, :] <= place[..., None], ends[None, None, :], -base * bt), axis=-1
    )
    reach = 2 * (DOC_MOST // bt // 2 + 1)
    back = blocks[:, None] - jnp.arange(reach, dtype=jnp.int32)[None, :]
    table = slot_of[jnp.maximum(back, 0)].reshape(-1)
    gap = blocks[:, None] - rel[None, :]
    inverse = jnp.where((gap >= 0) & (gap < reach), gap, reach).reshape(-1).astype(jnp.int32)
    first = blocks[:, None] * bt
    info = jnp.stack([start - first, place - first], axis=1)
    info = jnp.repeat(info, share, axis=2).astype(jnp.int32)

    kv = jnp.stack([keys, values]).reshape(2, own_blocks, bt, kv_heads, HEAD_SIZE)
    kv = kv.transpose(3, 0, 1, 2, 4)
    kv = kv.reshape(kv_heads // SIDE, SIDE, 2, own_blocks, bt, HEAD_SIZE)
    attended, query_grad, grad = attend(table, inverse, info, queries, out_grad, kv, split)
    grad = grad.transpose(1, 2, 3, 0, 4).reshape(2, tokens, kv_heads, HEAD_SIZE)
    return attended, query_grad, grad[0], grad[1]


def solution(mesh):
    spec = P(("ctx", "head"), None, None)
    return jax.shard_map(
        body,
        mesh=mesh,
        in_specs=(spec, spec, spec, spec, P(), P()),
        out_specs=(spec, spec, spec, spec),
        check_vma=False,
    )
```

```python
import functools
import math

import jax
import jax.numpy as jnp
from jax import lax
from jax.experimental import pallas as pl
from jax.experimental.pallas import tpu as pltpu
from jax.sharding import PartitionSpec as P

HEAD_SIZE = 128
BLOCK_TOKENS = 128
HOPS = 2
DOC_MOST = 1024
SIDE = 2
NEG_BIG = -1e30
SCALE = HEAD_SIZE ** (-0.5)
SCALE_LOG2 = SCALE * math.log2(math.e)

NN = (((1,), (0,)), ((), ()))
NT = (((1,), (1,)), ((), ()))
TN = (((0,), (0,)), ((), ()))


def dot(a, b, dims):
    return lax.dot_general(a, b, dims, preferred_element_type=jnp.float32)


def fused_kernel(tab_ref, inv_ref, info_ref, q_ref, g_ref, kv_ref, o_ref, dq_ref, dkv_ref, *scratch):
    s_scr, e_scr, s_top, e_top, out_acc, dq_acc, part, acc = (
        scratch[k * SIDE : (k + 1) * SIDE] for k in range(8)
    )
    near, land, stage, back_land, mate_land, own = scratch[8 * SIDE : 8 * SIDE + 6]
    send, recv, pass_send, back_send, back_recv, mate_send, mate_recv = scratch[8 * SIDE + 6 :]
    step, turn = pl.program_id(0), pl.program_id(1)
    steps, turns = pl.num_programs(0), pl.num_programs(1)
    bt = q_ref.shape[0]
    share = q_ref.shape[1] // SIDE
    rows = bt * share
    sides = range(SIDE)
    max_tiles = s_scr[0].shape[0]
    reach = 2 * max_tiles + 1
    own_blocks = kv_ref.shape[3]
    split, row = lax.axis_size("head"), lax.axis_size("ctx")
    me_head, me_ctx = lax.axis_index("head"), lax.axis_index("ctx")
    groups = (HOPS + 1) * split
    window_blocks = groups * own_blocks
    even = lax.rem(me_ctx, 2) == 0
    odd = jnp.logical_not(even)
    mesh_ids = pl.DeviceIdType.MESH

    def ahead(g):
        return {"ctx": lax.rem(me_ctx + g // split, row), "head": lax.rem(me_head + g % split, split)}

    def behind(g):
        return {
            "ctx": lax.rem(me_ctx + row - g // split, row),
            "head": lax.rem(me_head + split - g % split, split),
        }

    def has_ahead(g):
        return me_ctx + g // split < row

    def has_behind(g):
        return me_ctx >= g // split

    def forth(g, p):
        return pltpu.make_async_remote_copy(
            src_ref=kv_ref.at[p], dst_ref=land.at[p, g - 1],
            send_sem=send.at[p, g - 1], recv_sem=recv.at[p, g - 1],
            device_id=ahead(g), device_id_type=pl.DeviceIdType.MESH,
        )

    def home(g, p):
        return pltpu.make_async_remote_copy(
            src_ref=stage.at[p, g - 1], dst_ref=back_land.at[p, g - 1],
            send_sem=back_send.at[p, g - 1], recv_sem=back_recv.at[p, g - 1],
            device_id=behind(g), device_id_type=pl.DeviceIdType.MESH,
        )

    def passed(g, p):
        source = kv_ref.at[p] if g == split else land.at[p, g - split - 1]
        return pltpu.make_async_remote_copy(
            src_ref=source, dst_ref=land.at[p, g - 1],
            send_sem=pass_send.at[p, g - 1], recv_sem=recv.at[p, g - 1],
            device_id={"ctx": lax.rem(me_ctx + 1, row), "head": me_head}, device_id_type=mesh_ids,
        )

    def to_mate(g, p):
        return pltpu.make_async_remote_copy(
            src_ref=stage.at[p, g - 1], dst_ref=mate_land.at[p, g - 1],
            send_sem=mate_send.at[p, g - 1], recv_sem=mate_recv.at[p, g - 1],
            device_id={"ctx": lax.rem(me_ctx + row - 1, row), "head": me_head},
            device_id_type=mesh_ids,
        )

    def sends_forth(g):
        return has_ahead(g) if g < split else has_ahead(g) & (lax.rem(me_ctx + g // split, 2) == 0)

    def sends_home(g):
        return has_behind(g) if g < split else has_behind(g) & even

    def passes(g):
        return even & has_behind(g - split)

    def send_forth(p):
        for g in range(1, groups):
            @pl.when(sends_forth(g))
            def _():
                forth(g, p).start()

        @pl.when(even)
        def _():
            passed(split, p).start()

    def arrive(p):
        for g in range(1, groups):
            @pl.when(has_behind(g))
            def _():
                forth(g, p).wait_recv()

    def pass_on(p):
        @pl.when(even)
        def _():
            arrive(p)
        for g in range(split + 1, groups):
            @pl.when(passes(g))
            def _():
                passed(g, p).start()

    def settle(p):
        for g in range(groups - split):
            @pl.when(even & has_behind(g))
            def _():
                to_mate(g + split, p).wait_recv()
                other = mate_land[p, g + split - 1].astype(jnp.float32)
                if g == 0:
                    own[p] += other
                else:
                    stage[p, g - 1] = (stage[p, g - 1].astype(jnp.float32) + other).astype(
                        jnp.bfloat16
                    )
                    home(g, p).start()

    @pl.when((step == 0) & (turn == 0))
    def _():
        barrier = pltpu.get_barrier_semaphore()
        for g in range(1, groups):
            @pl.when(has_ahead(g))
            def _():
                pl.semaphore_signal(
                    barrier, inc=1, device_id=ahead(g), device_id_type=pl.DeviceIdType.MESH
                )

            if g >= split:
                @pl.when(has_behind(g))
                def _():
                    pl.semaphore_signal(
                        barrier, inc=1, device_id=behind(g), device_id_type=pl.DeviceIdType.MESH
                    )

        peers = split - 1
        for d in range(1, HOPS + 1):
            ends = (me_ctx + d < row).astype(jnp.int32) + (me_ctx >= d).astype(jnp.int32)
            peers = peers + split * ends
        pl.semaphore_wait(barrier, peers)

        send_forth(0)
        pass_on(0)
        for a in sides:
            part[a][:, reach] = jnp.zeros((2, bt, HEAD_SIZE), jnp.float32)

    @pl.when(turn == 0)
    def _():
        @pl.when(odd)
        def _():
            arrive(step)
        for a in sides:
            near[a, :, :own_blocks] = kv_ref[step, a]
        for g in range(1, groups):
            place_of = slice(g * own_blocks, (g + 1) * own_blocks)

            @pl.when(has_behind(g))
            def _():
                near[:, :, place_of] = land[step, g - 1]

            @pl.when(jnp.logical_not(has_behind(g)))
            def _():
                near[:, :, place_of] = jnp.zeros((SIDE, 2, own_blocks, bt, HEAD_SIZE), jnp.bfloat16)

        @pl.when(step == 0)
        def _():
            send_forth(1)

    @pl.when(turn == turns - 1)
    def _():
        @pl.when(step + 1 < steps)
        def _():
            pass_on(step + 1)

        @pl.when(step + 2 < steps)
        def _():
            send_forth(step + 2)

        @pl.when(step > 0)
        def _():
            settle(step - 1)

    query = [q_ref[:, a * share : (a + 1) * share, :].reshape(rows, HEAD_SIZE) for a in sides]
    query_t = [q.T for q in query]
    start = info_ref[turn, 0:1, :]
    place = info_ref[turn, 1:2, :]

    def tile_of(a, which, t):
        if t is None:
            return near[a, which, tab_ref[turn * reach]]
        low = tab_ref[turn * reach + 2 * t + 2]
        high = tab_ref[turn * reach + 2 * t + 1]
        return jnp.concatenate([near[a, which, low], near[a, which, high]], axis=0)

    def fold(x, op):
        return op(x.reshape(x.shape[0] // 8, 8, rows), axis=0)

    def scores(t):
        found = []
        count = bt if t is None else 2 * bt
        kpos = lax.broadcasted_iota(jnp.int32, (count, 1), 0)
        if t is None:
            keep = (kpos >= start) & (kpos <= place)
        else:
            keep = kpos - (2 * t + 2) * bt >= start
        for a in sides:
            s = dot(tile_of(a, 0, t), query_t[a], NN)
            s = jnp.where(keep, s, NEG_BIG)
            if t is None:
                s_top[a][...] = s
            else:
                s_scr[a][t] = s
            found.append(fold(s, jnp.max))
        return found

    best = scores(None)
    best = lax.fori_loop(
        0, max_tiles, lambda t, m: [jnp.maximum(x, y) for x, y in zip(m, scores(t))], best
    )
    top = [jnp.max(m, axis=0, keepdims=True) * SCALE_LOG2 for m in best]

    def weights(t, totals):
        new = []
        for a in sides:
            s = s_top[a][...] if t is None else s_scr[a][t]
            e = jnp.exp2(s * SCALE_LOG2 - top[a])
            low = e.astype(jnp.bfloat16)
            added = dot(tile_of(a, 1, t), low, TN)
            if t is None:
                e_top[a][...] = low
                out_acc[a][...] = added
                new.append(fold(e, jnp.sum))
            else:
                e_scr[a][t] = low
                out_acc[a][...] += added
                new.append(totals[a] + fold(e, jnp.sum))
        return new

    totals = lax.fori_loop(0, max_tiles, weights, weights(None, None))
    grad_t, grad, delta = [], [], []
    for a in sides:
        inv = 1.0 / jnp.sum(totals[a], axis=0, keepdims=True)
        mine = slice(a * share, (a + 1) * share)
        out_t = (out_acc[a][...] * inv).astype(jnp.bfloat16)
        o_ref[:, mine, :] = out_t.T.reshape(bt, share, HEAD_SIZE)
        raw = g_ref[:, mine, :].reshape(rows, HEAD_SIZE).T
        scaled = (raw.astype(jnp.float32) * inv).astype(jnp.bfloat16)
        product = scaled.astype(jnp.float32) * out_t.astype(jnp.float32)
        delta.append(jnp.sum(product, axis=0, keepdims=True))
        grad_t.append(scaled)
        grad.append(scaled.T)

    def back(t, carry):
        for a in sides:
            e = e_top[a][...] if t is None else e_scr[a][t]
            dp = dot(tile_of(a, 1, t), grad_t[a], NN)
            ds = (e.astype(jnp.float32) * (dp - delta[a])).astype(jnp.bfloat16)
            added = dot(tile_of(a, 0, t), ds, TN)
            dk = dot(ds, query[a], NN)
            dv = dot(e, grad[a], NN)
            if t is None:
                dq_acc[a][...] = added
                part[a][0, 0] = dk
                part[a][1, 0] = dv
            else:
                dq_acc[a][...] += added
                part[a][0, 2 * t + 2] = dk[:bt]
                part[a][0, 2 * t + 1] = dk[bt:]
                part[a][1, 2 * t + 2] = dv[:bt]
                part[a][1, 2 * t + 1] = dv[bt:]
        return carry

    back(None, 0)
    lax.fori_loop(0, max_tiles, back, 0)
    for a in sides:
        mine = slice(a * share, (a + 1) * share)
        dq = (dq_acc[a][...] * SCALE).astype(jnp.bfloat16)
        dq_ref[:, mine, :] = dq.T.reshape(bt, share, HEAD_SIZE)

    @pl.when(turn == 0)
    def _():
        for a in sides:
            acc[a][...] = jnp.zeros_like(acc[a])

    for w in range(window_blocks):
        found = inv_ref[turn * window_blocks + w]
        for a in sides:
            for which in range(2):
                acc[a][which, w] += part[a][which, found]

    def finish(p):
        for g in range(1, groups):
            comes = has_ahead(g)
            if g >= split:
                comes = comes & (lax.rem(me_ctx + g // split, 2) == 0)

            @pl.when(comes)
            def _():
                home(g, p).wait_recv()
                own[p] += back_land[p, g - 1].astype(jnp.float32)
        for a in sides:
            dkv_ref[p * SIDE + a] = own[p, a].astype(jnp.bfloat16)

    @pl.when(turn == turns - 1)
    def _():
        for a in sides:
            for which in range(2):
                factor = SCALE if which == 0 else 1.0
                for g in range(1, groups):
                    piece = acc[a][which, g * own_blocks : (g + 1) * own_blocks] * factor
                    stage[step, g - 1, a, which] = piece.astype(jnp.bfloat16)
                own[step, a, which] = acc[a][which, :own_blocks] * factor
        for g in range(1, groups):
            if g >= split:
                @pl.when(odd & has_behind(g))
                def _():
                    to_mate(g, step).start()

            @pl.when((even if g >= groups - split else odd) & sends_home(g))
            def _():
                home(g, step).start()

        @pl.when(step > 1)
        def _():
            finish(step - 2)

        @pl.when(step == steps - 1)
        def _():
            settle(step)
            finish(step - 1)
            finish(step)
            for p in range(send.shape[0]):
                for g in range(1, groups):
                    @pl.when(sends_forth(g))
                    def _():
                        forth(g, p).wait_send()

                    @pl.when(sends_home(g))
                    def _():
                        home(g, p).wait_send()

                    if g >= split:
                        @pl.when(passes(g))
                        def _():
                            passed(g, p).wait_send()

                        @pl.when(odd & has_behind(g))
                        def _():
                            to_mate(g, p).wait_send()


def attend(table, inverse, info, queries, out_grad, kv, split):
    tokens, heads, _ = queries.shape
    steps, _, _, own_blocks, bt, _ = kv.shape
    turns = own_blocks
    rows = info.shape[2]
    share = rows // bt
    max_tiles = DOC_MOST // bt // 2
    reach = 2 * max_tiles + 1
    groups = (HOPS + 1) * split
    window_blocks = groups * own_blocks
    by_head = pl.BlockSpec((bt, SIDE * share, HEAD_SIZE), lambda p, i: (i, p, 0))
    whole = pl.BlockSpec(memory_space=pltpu.VMEM)
    table_spec = pl.BlockSpec(memory_space=pltpu.SMEM)
    big = jax.ShapeDtypeStruct(queries.shape, jnp.bfloat16)
    pairs = steps * SIDE * turns * rows * reach * bt
    f32, low = jnp.float32, jnp.bfloat16
    piece = (SIDE, 2, own_blocks, bt, HEAD_SIZE)
    far = (steps, groups - 1) + piece
    sems = pltpu.SemaphoreType.DMA((steps, groups - 1))
    return pl.pallas_call(
        fused_kernel,
        grid=(steps, turns),
        in_specs=[table_spec, table_spec, whole, by_head, by_head, whole],
        out_specs=[by_head, by_head, whole],
        scratch_shapes=[pltpu.VMEM((max_tiles, 2 * bt, rows), f32)] * SIDE
        + [pltpu.VMEM((max_tiles, 2 * bt, rows), low)] * SIDE
        + [pltpu.VMEM((bt, rows), f32)] * SIDE
        + [pltpu.VMEM((bt, rows), low)] * SIDE
        + [pltpu.VMEM((HEAD_SIZE, rows), f32)] * (2 * SIDE)
        + [pltpu.VMEM((2, reach + 1, bt, HEAD_SIZE), f32)] * SIDE
        + [pltpu.VMEM((2, window_blocks, bt, HEAD_SIZE), f32)] * SIDE
        + [
            pltpu.VMEM((SIDE, 2, window_blocks, bt, HEAD_SIZE), low),
            pltpu.VMEM(far, low),
            pltpu.VMEM(far, low),
            pltpu.VMEM(far, low),
            pltpu.VMEM(far, low),
            pltpu.VMEM((steps,) + piece, f32),
            sems,
            sems,
            sems,
            sems,
            sems,
            sems,
            sems,
        ],
        out_shape=[big, big, jax.ShapeDtypeStruct((steps * SIDE,) + piece[1:], low)],
        compiler_params=pltpu.CompilerParams(
            collective_id=0, has_side_effects=True, vmem_limit_bytes=60 * 1024 * 1024
        ),
        cost_estimate=pl.CostEstimate(
            flops=12 * pairs * HEAD_SIZE,
            bytes_accessed=4 * queries.size * 2,
            transcendentals=pairs,
        ),
    )(table, inverse, info, queries, out_grad, kv)


def body(queries, keys, values, out_grad, doc_lengths, stored_block_order):
    tokens, heads, _ = queries.shape
    bt = min(BLOCK_TOKENS, tokens)
    pieces = BLOCK_TOKENS // bt
    stored_order = stored_block_order[:, None] * pieces + jnp.arange(pieces, dtype=jnp.int32)
    stored_order = stored_order.reshape(-1)
    kv_heads = keys.shape[1]
    share = heads // kv_heads
    own_blocks = tokens // bt
    split = lax.axis_size("head")
    me_head, me_ctx = lax.axis_index("head"), lax.axis_index("ctx")
    group = own_blocks * split
    window_blocks = (HOPS + 1) * group

    w = jnp.arange(window_blocks, dtype=jnp.int32)
    hop, turn, inner = w // group, (w % group) // own_blocks, w % own_blocks
    source = lax.rem(me_head - turn + split, split)
    stored = jnp.maximum(me_ctx - hop, 0) * group + source * own_blocks + inner
    rel = (HOPS - hop) * group + stored_order[stored] % group
    slot_of = jnp.sum(jnp.where(rel[None, :] == w[:, None], w[None, :], 0), axis=1).astype(jnp.int32)

    own = (me_ctx * split + me_head) * own_blocks
    base = (me_ctx - HOPS) * group
    blocks = lax.dynamic_slice_in_dim(stored_order, own, own_blocks, 0) - base
    place = blocks[:, None] * bt + jnp.arange(bt, dtype=jnp.int32)[None, :]
    ends = jnp.cumsum(doc_lengths).astype(jnp.int32) - base * bt
    start = jnp.max(
        jnp.where(ends[None, None, :] <= place[..., None], ends[None, None, :], -base * bt), axis=-1
    )
    reach = DOC_MOST // bt + 1
    back = blocks[:, None] - jnp.arange(reach, dtype=jnp.int32)[None, :]
    table = slot_of[jnp.maximum(back, 0)].reshape(-1)
    gap = blocks[:, None] - rel[None, :]
    inverse = jnp.where((gap >= 0) & (gap < reach), gap, reach).reshape(-1).astype(jnp.int32)
    first = blocks[:, None] * bt
    info = jnp.stack([start - first, place - first], axis=1)
    info = jnp.repeat(info, share, axis=2).astype(jnp.int32)

    kv = jnp.stack([keys, values]).reshape(2, own_blocks, bt, kv_heads, HEAD_SIZE)
    kv = kv.transpose(3, 0, 1, 2, 4)
    kv = kv.reshape(kv_heads // SIDE, SIDE, 2, own_blocks, bt, HEAD_SIZE)
    attended, query_grad, grad = attend(table, inverse, info, queries, out_grad, kv, split)
    grad = grad.transpose(1, 2, 3, 0, 4).reshape(2, tokens, kv_heads, HEAD_SIZE)
    return attended, query_grad, grad[0], grad[1]


def solution(mesh):
    spec = P(("ctx", "head"), None, None)
    return jax.shard_map(
        body,
        mesh=mesh,
        in_specs=(spec, spec, spec, spec, P(), P()),
        out_specs=(spec, spec, spec, spec),
        check_vma=False,
    )
```
